128 devices in a mesh: gx: 4 (over y), gy: 4 (over z), gz: 8 (over x, core).
Axes of the slice: x: 4, y: 4, z: 4, core: 2. Of those that a mesh axis runs over, the one named last changes fastest.
Arguments:
- position: float32 [16384, 3, 128], P(('gx', 'gy', 'gz')), may hold values from 0 to 8, as said below
- velocity: float32 [16384, 3, 128], P(('gx', 'gy', 'gz')), may hold values from -0.3 to 0.3
- particle_mass: float32 [16384, 128], P(('gx', 'gy', 'gz')), may hold values from 0.001953125 to 0.0078125
- send_first: int32 [128, 128, 4], P(('gx', 'gy', 'gz')), may hold values from -1 to 127, as said below
- neighbours_first: int32 [16384, 16], P(('gx', 'gy', 'gz')), may hold values from 0 to 639, as said below
- destination: int32 [16384], P(('gx', 'gy', 'gz')), may hold values from 0 to 16383, as said below
- send_second: int32 [128, 128, 4], P(('gx', 'gy', 'gz')), may hold values from -1 to 127, as said below
- neighbours_second: int32 [16384, 16], P(('gx', 'gy', 'gz')), may hold values from 0 to 639, as said below
Outputs:
- position_out: float32 [16384, 3, 128], P(('gx', 'gy', 'gz'))
- velocity_out: float32 [16384, 3, 128], P(('gx', 'gy', 'gz'))
- density_out: float32 [16384, 128], P(('gx', 'gy', 'gz'))
The draws below stay inside these ranges and needn't reach their ends.
Inputs may be any that keep to these rules, and one draw needn't show every extreme that they name: The particles of a block owned by the device at grid position (i_gx, i_gy, i_gz) lie in its box [i_gx, i_gx + 1] x [i_gy, i_gy + 1] x [i_gz, i_gz + 1], all of one block within a cube of side 1/2. `send_first`: only devices whose grid positions along gx, gy and gz differ by at most one in each (and are not the same) send ghosts to each other. The filled slots of one pair come first and hold distinct blocks; some pair fills all 4 slots. `send_second`: as for send_first, in the new layout. `neighbours_first`: entries name only the device's own blocks or filled ghost slots of send_first; the entries of a block are distinct and never the block itself. `neighbours_second`: entries name only the device's own blocks or filled ghost slots of send_second; the entries of a block are distinct and never the block itself. `destination`: A permutation of the 16384 positions; a block stays or moves to a device next to its owner along exactly one of gx, gy, gz; at most 2 blocks go from one device to another, and some pairs move exactly 2.
All inputs are finite; a program needn't handle non-finite values.
Results may differ from the reference program's by a relative error of at most 0.0001.
Values sent between devices are 32-bit elements; how exact they have to be, the bound alone decides.
No kernel may reach another device: no remote copies, remote signals or barrier semaphores. Data moves between devices by JAX's collectives and lax.ppermute only.
A program may use at most 128 MiB of HBM per device.

```python
import math
import jax
import jax.numpy as jnp
from jax import lax

PARTICLES = 128
NEIGHBOURS = 16
BLOCKS = 128
GHOST_CAP = 4
MOVE_CAP = 2
ALL_BLOCKS = 16384
N_GX = 4
N_GY = 4
N_GZ = 8


def grid_places():
    devices = N_GX * N_GY * N_GZ
    index = jnp.arange(devices, dtype=jnp.int32)
    along = (index // (N_GY * N_GZ), index // N_GZ % N_GY, index % N_GZ)
    return (index, along)


def block_cells(key):
    index, along = grid_places()
    devices = N_GX * N_GY * N_GZ
    scores = jax.random.randint(jax.random.fold_in(key, 21), (devices, BLOCKS), 0, 1 << 14) * BLOCKS
    ordered = jnp.argsort(scores + jnp.arange(BLOCKS, dtype=jnp.int32)[None, :], axis=1).astype(jnp.int32)
    octant = ordered % 8
    first = 2 * along[0][:, None] + octant // 4
    second = 2 * along[1][:, None] + octant // 2 % 2
    third = 2 * along[2][:, None] + octant % 2
    return jnp.stack([first, second, third], axis=2).astype(jnp.int32)


def draw_destination(key, part):
    base = jax.random.fold_in(key, 13)
    index, along = grid_places()
    devices = N_GX * N_GY * N_GZ
    extents = (N_GX, N_GY, N_GZ)
    strides = (N_GY * N_GZ, N_GZ, 1)
    cells = block_cells(key)
    block_index = jnp.arange(BLOCKS, dtype=jnp.int32)
    target = index[:, None] * BLOCKS + block_index[None, :]
    taken = jnp.zeros((devices, BLOCKS), jnp.int32)
    for rounds in range(6):
        axis_number = rounds // 2
        parity = rounds % 2
        place = along[axis_number]
        partner_place = jnp.where((place - parity) % 2 == 0, place + 1, place - 1)
        exists = (partner_place >= 0) & (partner_place < extents[axis_number])
        partner = jnp.clip(index + (partner_place - place) * strides[axis_number], 0, devices - 1)
        local_cell = cells[:, :, axis_number] - 2 * place[:, None]
        facing = jnp.where((partner_place > place)[:, None], local_cell == 1, local_cell == 0)
        ranking = jax.random.randint(jax.random.fold_in(base, 20 + rounds), (devices, BLOCKS), 0, 1 << 14) * BLOCKS
        ranking = ranking + block_index[None, :] + jnp.where(facing, 0, 1 << 28) + taken * (1 << 29)
        picked = jnp.argsort(ranking, axis=1).astype(jnp.int32)[:, :MOVE_CAP]
        amount = jax.random.randint(jax.random.fold_in(base, rounds + 1), (devices,), 1, MOVE_CAP + 1)
        if rounds == 0:
            amount = jnp.full((devices,), MOVE_CAP, jnp.int32)
        pair_amount = amount[jnp.minimum(index, partner)]
        for offset in range(MOVE_CAP):
            mine = picked[:, offset]
            theirs = picked[partner, offset]
            active = exists & (offset < pair_amount)
            target = target.at[index, mine].set(jnp.where(active, partner * BLOCKS + theirs, target[index, mine]))
            taken = taken.at[index, mine].set(jnp.maximum(taken[index, mine], active.astype(jnp.int32)))
    return target.reshape(devices * BLOCKS).astype(jnp.int32)


def moved_cells(key):
    cells = block_cells(key)
    devices = N_GX * N_GY * N_GZ
    destination = draw_destination(key, 0)
    flat = jnp.zeros((devices * BLOCKS, 3), jnp.int32).at[destination].set(cells.reshape(devices * BLOCKS, 3))
    return flat.reshape(devices, BLOCKS, 3)


def ghost_tables(key, which, cells):
    base = jax.random.fold_in(key, which)
    index, along = grid_places()
    devices = N_GX * N_GY * N_GZ
    near = (jnp.abs(along[0][:, None] - along[0][None, :]) <= 1) & (jnp.abs(along[1][:, None] - along[1][None, :]) <= 1)
    near = near & (jnp.abs(along[2][:, None] - along[2][None, :]) <= 1) & (index[:, None] != index[None, :])
    corner = jnp.stack(along, axis=1)
    lower = 2 * corner - 1
    upper = 2 * corner + 2
    eligible = (cells[:, None, :, :] >= lower[None, :, None, :]) & (cells[:, None, :, :] <= upper[None, :, None, :])
    eligible = jnp.all(eligible, axis=3)
    reach = jnp.sum(eligible.astype(jnp.int32), axis=2)
    amount = jax.random.randint(jax.random.fold_in(base, 1), (devices, devices), 1, GHOST_CAP + 1)
    forced = (index[:, None] == 1) & (index[None, :] == 0) | (index[:, None] == 0) & (index[None, :] == 1)
    amount = jnp.minimum(jnp.where(forced, GHOST_CAP, amount), reach) * near.astype(jnp.int32)
    block_index = jnp.arange(BLOCKS, dtype=jnp.int32)
    scores = jax.random.randint(jax.random.fold_in(base, 2), (devices, devices, BLOCKS), 0, 1 << 14) * BLOCKS
    scores = scores + block_index[None, None, :] + jnp.where(eligible, 0, 1 << 28)
    chosen = jnp.argsort(scores, axis=2).astype(jnp.int32)[:, :, :GHOST_CAP]
    slot_index = jnp.arange(GHOST_CAP, dtype=jnp.int32)
    sender = jnp.where(slot_index[None, None, :] < amount[:, :, None], chosen, -1).astype(jnp.int32)
    received = jnp.transpose(sender, (1, 0, 2))
    ghost_cell = cells[index[None, :, None], jnp.maximum(received, 0)]
    entry_cells = jnp.concatenate([cells, ghost_cell.reshape(devices, devices * GHOST_CAP, 3)], axis=1)
    filled = jnp.concatenate([jnp.ones((devices, BLOCKS), bool), (received >= 0).reshape(devices, devices * GHOST_CAP)], axis=1)
    width = BLOCKS + devices * GHOST_CAP
    entry_index = jnp.arange(width, dtype=jnp.int32)
    adjacent = filled[:, None, :] & jnp.ones((devices, BLOCKS, width), bool)
    for axis_number in range(3):
        spacing = cells[:, :, None, axis_number] - entry_cells[:, None, :, axis_number]
        adjacent = adjacent & (jnp.abs(spacing) <= 1)
    host_score = jax.random.randint(jax.random.fold_in(base, 3), (devices, BLOCKS, width), 0, 1 << 14) * BLOCKS
    host_score = host_score + block_index[None, :, None] + jnp.where(adjacent, 1 << 28, 0)
    host_block = jnp.argsort(host_score, axis=1).astype(jnp.int32)[:, BLOCKS - 1, :]
    designated = (block_index[None, :, None] == host_block[:, None, :]) & adjacent & (entry_index >= BLOCKS)[None, None, :]
    own_entry = entry_index[None, None, :] == block_index[None, :, None]
    entry_class = jnp.where(designated, 0, jnp.where(adjacent, 1, 2))
    entry_class = jnp.where(jnp.logical_not(filled)[:, None, :], 3, entry_class)
    entry_class = jnp.where(own_entry, 4, entry_class)
    ranking = jax.random.randint(jax.random.fold_in(base, 4), (devices, BLOCKS, width), 0, 1 << 12) * width
    ranking = entry_class * (1 << 26) + ranking + entry_index[None, None, :]
    entries = jnp.argsort(ranking, axis=2).astype(jnp.int32)[:, :, :NEIGHBOURS]
    return (sender, entries.reshape(devices * BLOCKS, NEIGHBOURS).astype(jnp.int32))


def draw_position(key, part):
    devices = N_GX * N_GY * N_GZ
    cells = block_cells(key).reshape(devices * BLOCKS, 3).astype(jnp.float32)
    base = jax.random.fold_in(key, 22)
    shape = (devices * BLOCKS, 3, PARTICLES)
    jitter = jax.random.uniform(jax.random.fold_in(base, 1), shape, jnp.float32)
    return ((cells[:, :, None] + jitter) * 0.5).astype(jnp.float32)


def draw_send_first(key, part):
    return ghost_tables(key, 11, block_cells(key))[0]


def draw_neighbours_first(key, part):
    return ghost_tables(key, 11, block_cells(key))[1]


def draw_send_second(key, part):
    return ghost_tables(key, 12, moved_cells(key))[0]


def draw_neighbours_second(key, part):
    return ghost_tables(key, 12, moved_cells(key))[1]


def block_scale(key, dims, cuts, least, top_value):
    level = 1.0
    for dim, shards_of in cuts:
        heights = jax.random.uniform(jax.random.fold_in(jax.random.fold_in(key, 6), dim), (shards_of,), jnp.float32, least / len(cuts), top_value / len(cuts))
        level = level * jnp.repeat(jnp.exp(heights), dims[dim] // shards_of).reshape((-1,) + (1,) * (len(dims) - 1 - dim))
    return level


def setup_inputs(seed: int = 0) -> dict:
    splits = jax.random.split(jax.random.key(seed), 9)
    position = draw_position(jax.random.fold_in(splits[8], 71), 0)
    velocity = jnp.clip(jax.random.uniform(splits[1], (ALL_BLOCKS, 3, PARTICLES), jnp.float32, -0.3, 0.3) * block_scale(splits[1], (ALL_BLOCKS, 3, PARTICLES), ((0, 128),), -0.4, 0.0), -0.3, 0.3)
    particle_mass = jnp.clip(jnp.exp(math.log(0.0078125) - 1.3862944 * jax.random.uniform(splits[2], (ALL_BLOCKS, PARTICLES), jnp.float32) ** block_scale(splits[2], (ALL_BLOCKS, PARTICLES), ((0, 128),), -0.2, 0.2)), 0.001953125, 0.0078125)
    send_first = draw_send_first(jax.random.fold_in(splits[8], 71), 0)
    neighbours_first = draw_neighbours_first(jax.random.fold_in(splits[8], 71), 0)
    destination = draw_destination(jax.random.fold_in(splits[8], 71), 0)
    send_second = draw_send_second(jax.random.fold_in(splits[8], 71), 0)
    neighbours_second = draw_neighbours_second(jax.random.fold_in(splits[8], 71), 0)
    return {"position": position, "velocity": velocity, "particle_mass": particle_mass, "send_first": send_first, "neighbours_first": neighbours_first, "destination": destination, "send_second": send_second, "neighbours_second": neighbours_second}


smooth_len = 0.5
time_step = 0.25


def pair_density(home_points, away_points, away_mass):
    offset = home_points[:, :, :, None] - away_points[:, :, None, :]
    squared = jnp.sum(offset * offset, axis=1)
    kernel = jnp.maximum(1.0 - squared / (smooth_len * smooth_len), 0.0)
    return jnp.sum(away_mass[:, None, :] * (kernel * kernel * kernel), axis=2)


def pair_force(home_points, home_term, away_points, away_mass, away_term):
    offset = home_points[:, :, :, None] - away_points[:, :, None, :]
    squared = jnp.sum(offset * offset, axis=1)
    kernel = jnp.maximum(1.0 - squared / (smooth_len * smooth_len), 0.0)
    weight = away_mass[:, None, :] * (home_term[:, :, None] + away_term[:, None, :]) * kernel * kernel
    return (6.0 / (smooth_len * smooth_len)) * jnp.sum(weight[:, None, :, :] * offset, axis=3)


def pressure_term(density):
    return jnp.exp(jnp.log(density) * (-1.0 / 3.0))


def table_density(home_points, home_mass, all_points, all_mass, lookup):
    initial = pair_density(home_points, home_points, home_mass)

    def add_column(column, running):
        picked = lookup[:, column]
        return running + pair_density(home_points, all_points[picked], all_mass[picked])

    return lax.fori_loop(0, lookup.shape[1], add_column, initial)


def table_force(home_points, home_mass, home_term, all_points, all_mass, all_term, lookup):
    initial = pair_force(home_points, home_term, home_points, home_mass, home_term)

    def add_column(column, running):
        picked = lookup[:, column]
        return running + pair_force(home_points, home_term, all_points[picked], all_mass[picked], all_term[picked])

    return lax.fori_loop(0, lookup.shape[1], add_column, initial)


def global_rows(sender, neighbours):
    total_blocks = neighbours.shape[0]
    owner_device = jnp.arange(total_blocks, dtype=jnp.int32) // BLOCKS
    remote = jnp.maximum(neighbours - BLOCKS, 0)
    source = remote // GHOST_CAP
    within = remote % GHOST_CAP
    listed = sender[source, owner_device[:, None], within]
    far_row = jnp.where(listed >= 0, source * BLOCKS + listed, total_blocks)
    return jnp.where(neighbours < BLOCKS, owner_device[:, None] * BLOCKS + neighbours, far_row).astype(jnp.int32)


def sph_forces(points, weights, sender, neighbours):
    total_blocks = points.shape[0]
    groups = total_blocks // BLOCKS
    lookup = global_rows(sender, neighbours)
    all_points = jnp.concatenate([points, jnp.zeros((1,) + points.shape[1:], jnp.float32)], axis=0)
    all_mass = jnp.concatenate([weights, jnp.zeros((1, weights.shape[1]), jnp.float32)], axis=0)
    grouped_points = points.reshape((groups, BLOCKS) + points.shape[1:])
    grouped_mass = weights.reshape(groups, BLOCKS, weights.shape[1])
    grouped_rows = lookup.reshape(groups, BLOCKS, lookup.shape[1])

    def density_group(packed):
        return table_density(packed[0], packed[1], all_points, all_mass, packed[2])

    density = lax.map(density_group, (grouped_points, grouped_mass, grouped_rows)).reshape(weights.shape)
    all_rho = jnp.concatenate([density, jnp.ones((1, density.shape[1]), jnp.float32)], axis=0)
    all_term = pressure_term(all_rho)
    grouped_term = all_term[:total_blocks].reshape(groups, BLOCKS, weights.shape[1])

    def force_group(packed):
        return table_force(packed[0], packed[1], packed[3], all_points, all_mass, all_term, packed[2])

    acceleration = lax.map(force_group, (grouped_points, grouped_mass, grouped_rows, grouped_term)).reshape(points.shape)
    return density, acceleration


def reference(position, velocity, particle_mass, send_first, neighbours_first, destination, send_second, neighbours_second):
    density, acceleration = sph_forces(position, particle_mass, send_first, neighbours_first)
    velocity = velocity + time_step * acceleration
    position = position + time_step * velocity
    position = jnp.zeros_like(position).at[destination].set(position)
    velocity = jnp.zeros_like(velocity).at[destination].set(velocity)
    moved_mass = jnp.zeros_like(particle_mass).at[destination].set(particle_mass)
    density, acceleration = sph_forces(position, moved_mass, send_second, neighbours_second)
    velocity = velocity + time_step * acceleration
    position = position + time_step * velocity
    return position, velocity, density
```

```python
import jax
import jax.numpy as jnp
from jax import lax
from jax.experimental import pallas as pl
from jax.experimental.pallas import tpu as pltpu
from jax.sharding import PartitionSpec as P

AXES = ("gx", "gy", "gz")
BLOCKS = 128
WIDTH = 128
GHOST_CAP = 4
MOVE_CAP = 2
NEIGHBOURS = 16
CODES = 27
STORED = BLOCKS + CODES * GHOST_CAP
TERMS = 48
time_step = 0.25
VMEM_LIMIT = 60 << 20

f32 = jnp.float32
bf16 = jnp.bfloat16
VMEM = pl.BlockSpec(memory_space=pltpu.VMEM)
SMEM = pl.BlockSpec(memory_space=pltpu.SMEM)


def shape(*dims, dtype=f32):
    return jax.ShapeDtypeStruct(dims, dtype)


def call(kernel, name, in_specs, out_shape, scratch=()):
    many = isinstance(out_shape, (list, tuple))
    return pl.pallas_call(
        kernel,
        in_specs=in_specs,
        out_specs=[VMEM] * len(out_shape) if many else VMEM,
        out_shape=out_shape,
        scratch_shapes=list(scratch),
        compiler_params=pltpu.CompilerParams(vmem_limit_bytes=VMEM_LIMIT),
        name=name,
    )


def near_device(place, code):
    ix = jnp.clip(place[1] + code // 9 - 1, 0, place[4] - 1)
    iy = jnp.clip(place[2] + code // 3 % 3 - 1, 0, place[5] - 1)
    iz = jnp.clip(place[3] + code % 3 - 1, 0, place[6] - 1)
    return (ix * place[5] + iy) * place[6] + iz


def fill_sends(place, send, out, load):
    def one(code, carry):
        device = near_device(place, code)
        for slot in range(GHOST_CAP):
            row = jnp.maximum(send[device, slot], 0)
            out[device, slot] = load(row)
        return carry

    lax.fori_loop(0, CODES, one, 0)


def parts_of(value):
    high = value.astype(bf16).astype(f32)
    rest = value - high
    middle = rest.astype(bf16).astype(f32)
    return high, middle, rest - middle


def away_terms(rows):
    high, middle, low = parts_of(rows)
    return jnp.concatenate([high, middle, high, middle, low, high], axis=0).astype(bf16)


def home_terms(rows):
    high, middle, low = parts_of(rows)
    return jnp.concatenate([high, high, middle, middle, high, low], axis=0)


def prepare(place, stored, points, mass, away_density, away_force, local):
    axis = [points[k : k + 1] - (place[1 + k].astype(f32) + 0.5) for k in range(3)]
    square = axis[0] * axis[0] + axis[1] * axis[1] + axis[2] * axis[2]
    one = jnp.ones_like(square)
    nil = jnp.zeros_like(square)
    away = jnp.concatenate(
        [1.0 - 4.0 * square] + [8.0 * a for a in axis] + [-4.0 * one, nil, nil, nil], axis=0
    )
    away_density[stored] = away_terms(jnp.exp(jnp.log(mass) * (1.0 / 3.0)) * away)
    away_force[stored] = away_terms(jnp.sqrt(mass) * away)
    home = jnp.concatenate([one] + axis + [square, nil, nil, nil], axis=0)
    local[stored] = jnp.concatenate(axis + [one, one, one, one, one], axis=0)
    return home


def lane_sums(values):
    return jnp.sum(values.T, axis=0, keepdims=True)


def density_kernel(place, lookup, send, points, mass, ghosts, rho, rho_send, away_force, home, local, away_density):
    def own(block, carry):
        rows = prepare(place, block, points[block], mass[pl.ds(block, 1)], away_density, away_force, local)
        home[block] = home_terms(rows).T.astype(bf16)
        return carry

    lax.fori_loop(0, BLOCKS, own, 0)

    def other(code, carry):
        device = near_device(place, code)
        for slot in range(GHOST_CAP):
            block = ghosts[device, slot]
            prepare(place, BLOCKS + code * GHOST_CAP + slot, block[0:3], block[3:4], away_density, away_force, local)
        return carry

    lax.fori_loop(0, CODES, other, 0)

    unroll = 4

    def some(step, carry):
        for part in range(unroll):
            block = step * unroll + part
            left = home[block]
            names = [block] + [lookup[block, n] for n in range(NEIGHBOURS)]
            total = jnp.zeros((WIDTH, WIDTH), f32)
            for first in range(0, NEIGHBOURS + 1, 2):
                some_names = names[first : first + 2]
                right = jnp.concatenate([away_density[n] for n in some_names], axis=1)
                kernel = jnp.maximum(jnp.dot(left, right, preferred_element_type=f32), 0.0)
                cube = kernel * kernel * kernel
                for k in range(len(some_names)):
                    total = total + cube[:, k * WIDTH : (k + 1) * WIDTH]
            rho[pl.ds(block, 1)] = lane_sums(total)
        return carry

    lax.fori_loop(0, BLOCKS // unroll, some, 0)

    def one(code, carry):
        device = near_device(place, code)
        for slot in range(GHOST_CAP):
            row = jnp.maximum(send[device, slot], 0)
            rho_send[device, pl.ds(slot, 1)] = rho[pl.ds(row, 1)]
        return carry

    lax.fori_loop(0, CODES, one, 0)


def pressure(density):
    return jnp.exp(jnp.log(density) * (-1.0 / 3.0))


def force_kernel(place, lookup, rho, rho_ghosts, away_force, home, local, emit):
    def own(block, carry):
        local[block, 3:4] = pressure(rho[pl.ds(block, 1)])
        return carry

    lax.fori_loop(0, BLOCKS, own, 0)

    def other(code, carry):
        device = near_device(place, code)
        values = pressure(rho_ghosts[device])
        for slot in range(GHOST_CAP):
            local[BLOCKS + code * GHOST_CAP + slot, 3:4] = values[slot : slot + 1]
        return carry

    lax.fori_loop(0, CODES, other, 0)

    unroll = 2

    def some(step, carry):
        for part in range(unroll):
            block = step * unroll + part
            left = home[block]
            mine = local[block]
            names = [block] + [lookup[block, n] for n in range(NEIGHBOURS)]
            own_term = jnp.broadcast_to(mine[3:4], (WIDTH, WIDTH)).T
            total = [jnp.zeros((WIDTH, WIDTH), f32) for _ in range(4)]
            for first in range(0, NEIGHBOURS + 1, 2):
                some_names = names[first : first + 2]
                right = jnp.concatenate([away_force[n] for n in some_names], axis=1)
                kernel = jnp.maximum(jnp.dot(left, right, preferred_element_type=f32), 0.0)
                for k, name in enumerate(some_names):
                    this = kernel[:, k * WIDTH : (k + 1) * WIDTH]
                    weight = this * this * (own_term + local[name, 3:4])
                    total[3] = total[3] + weight
                    for c in range(3):
                        total[c] = total[c] + weight * local[name, c : c + 1]
            whole = lane_sums(total[3])
            pull = [24.0 * (mine[c : c + 1] * whole - lane_sums(total[c])) for c in range(3)]
            emit(block, jnp.concatenate(pull, axis=0))
        return carry

    lax.fori_loop(0, BLOCKS // unroll, some, 0)


def move_kernel(place, target, state, stay, outbox):
    outbox[...] = jnp.zeros_like(outbox)

    def one(block, counts):
        goal = target[block]
        device = goal // BLOCKS
        spot = goal % BLOCKS
        rows = state[block]
        here = device == place[0]

        @pl.when(here)
        def _():
            stay[spot] = rows

        dx = device // (place[5] * place[6]) - place[1]
        dy = device // place[6] % place[5] - place[2]
        dz = device % place[6] - place[3]
        heading = jnp.where(
            dx != 0,
            jnp.where(dx > 0, 1, 0),
            jnp.where(dy != 0, jnp.where(dy > 0, 3, 2), jnp.where(dz > 0, 5, 4)),
        )
        used = counts[0]
        for k in range(1, 6):
            used = jnp.where(heading == k, counts[k], used)

        @pl.when(jnp.logical_not(here))
        def _():
            slot = heading * MOVE_CAP + jnp.minimum(used, MOVE_CAP - 1)
            outbox[slot, 0:7] = rows[0:7]
            outbox[slot, 7:8] = jnp.full((1, WIDTH), spot + 1, jnp.int32).astype(f32)

        gone = jnp.where(here, 0, 1)
        return tuple(counts[k] + jnp.where(heading == k, gone, 0) for k in range(6))

    lax.fori_loop(0, BLOCKS, one, (jnp.int32(0),) * 6)


def merge_kernel(place, labels, send, stay, arrived, points, velocity, mass, ghost_send):
    def put(spot, rows):
        points[spot] = rows[0:3]
        velocity[spot] = rows[3:6]
        mass[pl.ds(spot, 1)] = rows[6:7]

    def copy(block, carry):
        put(block, stay[block])
        return carry

    lax.fori_loop(0, BLOCKS, copy, 0)
    for k in range(6 * MOVE_CAP):

        @pl.when(labels[k] > 0)
        def _():
            put(labels[k] - 1, arrived[k])

    def load(row):
        return jnp.concatenate([points[row], mass[pl.ds(row, 1)]], axis=0)

    fill_sends(place, send, ghost_send, load)


def pack_kernel(place, send, points, mass, ghost_send):
    def load(row):
        return jnp.concatenate([points[row], mass[pl.ds(row, 1)]], axis=0)

    fill_sends(place, send, ghost_send, load)


def last_force_kernel(place, lookup, rho, rho_ghosts, away_force, home, local_in, points, velocity, points_out, velocity_out, local):
    local[...] = local_in[...]

    def emit(block, pull):
        speed = velocity[block] + time_step * pull
        velocity_out[block] = speed
        points_out[block] = points[block] + time_step * speed

    force_kernel(place, lookup, rho, rho_ghosts, away_force, home, local, emit)


def table_rows(neighbours):
    size_y = lax.axis_size("gy")
    size_z = lax.axis_size("gz")
    remote = jnp.maximum(neighbours - BLOCKS, 0)
    source = remote // GHOST_CAP
    within = remote % GHOST_CAP
    code = (source // (size_y * size_z) - lax.axis_index("gx") + 1) * 9
    code = code + (source // size_z % size_y - lax.axis_index("gy") + 1) * 3
    code = code + (source % size_z - lax.axis_index("gz") + 1)
    return jnp.where(neighbours < BLOCKS, neighbours, BLOCKS + code * GHOST_CAP + within)


def to_all(values):
    return lax.all_to_all(values, AXES, 0, 0, tiled=True)


def shifted(values, axis, step):
    count = lax.axis_size(axis)
    pairs = [(i, i + step) for i in range(count) if 0 <= i + step < count]
    return lax.ppermute(values, axis, pairs)


def densities(place, lookup, send, points, mass, ghost_send, devices):
    ghosts = to_all(ghost_send)
    return call(
        density_kernel,
        "density",
        [SMEM] * 3 + [VMEM] * 3,
        [
            shape(BLOCKS, WIDTH),
            shape(devices, GHOST_CAP, WIDTH),
            shape(STORED, TERMS, WIDTH, dtype=bf16),
            shape(BLOCKS, WIDTH, TERMS, dtype=bf16),
            shape(STORED, 8, WIDTH),
        ],
        [pltpu.VMEM((STORED, TERMS, WIDTH), bf16)],
    )(place, lookup, send, points, mass, ghosts)


def per_device(position, velocity, mass, send_first, neighbours_first, destination, send_second, neighbours_second):
    sizes = [lax.axis_size(a) for a in AXES]
    devices = sizes[0] * sizes[1] * sizes[2]
    place = jnp.stack(
        [lax.axis_index(AXES).astype(jnp.int32)]
        + [lax.axis_index(a).astype(jnp.int32) for a in AXES]
        + [jnp.int32(s) for s in sizes]
    )
    send_first, send_second = send_first[0], send_second[0]
    lookup_first, lookup_second = table_rows(neighbours_first), table_rows(neighbours_second)
    ghost_shape = shape(devices, GHOST_CAP, 4, WIDTH)
    ghost_send = call(pack_kernel, "pack", [SMEM] * 2 + [VMEM] * 2, ghost_shape)(place, send_first, position, mass)
    rho, rho_send, away_force, home, local = densities(
        place, lookup_first, send_first, position, mass, ghost_send, devices
    )
    rho_ghosts = to_all(rho_send)

    def first(place, lookup, rho, rho_ghosts, away_force, home, local_in, points, velocity, mass, state, local):
        local[...] = local_in[...]

        def emit(block, pull):
            speed = velocity[block] + time_step * pull
            state[block, 0:3] = points[block] + time_step * speed
            state[block, 3:6] = speed
            state[block, 6:7] = mass[pl.ds(block, 1)]

        force_kernel(place, lookup, rho, rho_ghosts, away_force, home, local, emit)

    state = call(
        first, "force", [SMEM] * 2 + [VMEM] * 8, shape(BLOCKS, 8, WIDTH), [pltpu.VMEM((STORED, 8, WIDTH), f32)]
    )(place, lookup_first, rho, rho_ghosts, away_force, home, local, position, velocity, mass)
    stay, outbox = call(
        move_kernel,
        "move",
        [SMEM] * 2 + [VMEM],
        [shape(BLOCKS, 8, WIDTH), shape(6 * MOVE_CAP, 8, WIDTH)],
    )(place, destination, state)
    boxes = outbox.reshape(6, MOVE_CAP, 8, WIDTH)
    arrived = jnp.concatenate(
        [shifted(boxes[2 * k + way], axis, 2 * way - 1) for k, axis in enumerate(AXES) for way in (0, 1)], axis=0
    )
    labels = arrived[:, 7, 0].astype(jnp.int32)
    position, velocity, mass, ghost_send = call(
        merge_kernel,
        "merge",
        [SMEM] * 3 + [VMEM] * 2,
        [shape(BLOCKS, 3, WIDTH), shape(BLOCKS, 3, WIDTH), shape(BLOCKS, WIDTH), ghost_shape],
    )(place, labels, send_second, stay, arrived)
    rho, rho_send, away_force, home, local = densities(
        place, lookup_second, send_second, position, mass, ghost_send, devices
    )
    rho_ghosts = to_all(rho_send)
    position, velocity = call(
        last_force_kernel,
        "last_force",
        [SMEM] * 2 + [VMEM] * 7,
        [shape(BLOCKS, 3, WIDTH), shape(BLOCKS, 3, WIDTH)],
        [pltpu.VMEM((STORED, 8, WIDTH), f32)],
    )(place, lookup_second, rho, rho_ghosts, away_force, home, local, position, velocity)
    return position, velocity, rho


def solution(mesh):
    along = P(AXES)
    return jax.shard_map(
        per_device, mesh=mesh, in_specs=(along,) * 8, out_specs=(along,) * 3, check_vma=False
    )
```

```python
import jax
import jax.numpy as jnp
from jax import lax
from jax.experimental import pallas as pl
from jax.experimental.pallas import tpu as pltpu
from jax.sharding import PartitionSpec as P

AXES = ("gx", "gy", "gz")
BLOCKS = 128
WIDTH = 128
GHOST_CAP = 4
MOVE_CAP = 2
NEIGHBOURS = 16
CODES = 27
STORED = BLOCKS + CODES * GHOST_CAP
TERMS = 48
time_step = 0.25
VMEM_LIMIT = 60 << 20

f32 = jnp.float32
bf16 = jnp.bfloat16
VMEM = pl.BlockSpec(memory_space=pltpu.VMEM)
SMEM = pl.BlockSpec(memory_space=pltpu.SMEM)


def shape(*dims, dtype=f32):
    return jax.ShapeDtypeStruct(dims, dtype)


def call(kernel, name, in_specs, out_shape, scratch=(), cost=None):
    many = isinstance(out_shape, (list, tuple))
    return pl.pallas_call(
        kernel,
        in_specs=in_specs,
        out_specs=[VMEM] * len(out_shape) if many else VMEM,
        out_shape=out_shape,
        scratch_shapes=list(scratch),
        compiler_params=pltpu.CompilerParams(vmem_limit_bytes=VMEM_LIMIT),
        cost_estimate=cost and pl.CostEstimate(flops=cost[0], bytes_accessed=cost[1], transcendentals=0),
        name=name,
    )


def near_device(place, code):
    ix = jnp.clip(place[1] + code // 9 - 1, 0, place[4] - 1)
    iy = jnp.clip(place[2] + code // 3 % 3 - 1, 0, place[5] - 1)
    iz = jnp.clip(place[3] + code % 3 - 1, 0, place[6] - 1)
    return (ix * place[5] + iy) * place[6] + iz


def fill_sends(place, send, out, load):
    def one(code, carry):
        device = near_device(place, code)
        for slot in range(GHOST_CAP):
            row = jnp.maximum(send[device, slot], 0)
            out[device, slot] = load(row)
        return carry

    lax.fori_loop(0, CODES, one, 0)


def parts_of(value):
    high = value.astype(bf16).astype(f32)
    rest = value - high
    middle = rest.astype(bf16).astype(f32)
    return high, middle, rest - middle


def away_terms(rows):
    high, middle, low = parts_of(rows)
    return jnp.concatenate([high, middle, high, middle, low, high], axis=0).astype(bf16)


def home_terms(rows):
    high, middle, low = parts_of(rows)
    return jnp.concatenate([high, high, middle, middle, high, low], axis=0)


def prepare(place, stored, points, mass, away_density, away_force, local):
    axis = [points[k : k + 1] - (place[1 + k].astype(f32) + 0.5) for k in range(3)]
    square = axis[0] * axis[0] + axis[1] * axis[1] + axis[2] * axis[2]
    one = jnp.ones_like(square)
    nil = jnp.zeros_like(square)
    away = jnp.concatenate(
        [1.0 - 4.0 * square] + [8.0 * a for a in axis] + [-4.0 * one, nil, nil, nil], axis=0
    )
    away_density[stored] = away_terms(jnp.exp(jnp.log(mass) * (1.0 / 3.0)) * away)
    away_force[stored] = away_terms(jnp.sqrt(mass) * away)
    home = jnp.concatenate([one] + axis + [square, nil, nil, nil], axis=0)
    local[stored] = jnp.concatenate(axis + [one, one, one, one, one], axis=0)
    return home


def lane_sums(values):
    return jnp.sum(values.T, axis=0, keepdims=True)


def own_kernel(place, points, mass, away_density, away_force, home, local):
    def own(block, carry):
        rows = prepare(place, block, points[block], mass[pl.ds(block, 1)], away_density, away_force, local)
        home[block] = home_terms(rows).T.astype(bf16)
        return carry

    lax.fori_loop(0, BLOCKS, own, 0, unroll=4)


def density_kernel(
    place, lookup, send, ghosts, own_density, own_force, home, own_local, rho, rho_send, away_force, local, away_density
):
    away_density[0:BLOCKS] = own_density[...]
    away_force[0:BLOCKS] = own_force[...]
    local[0:BLOCKS] = own_local[...]

    def other(code, carry):
        device = near_device(place, code)
        for slot in range(GHOST_CAP):
            block = ghosts[device, slot]
            prepare(place, BLOCKS + code * GHOST_CAP + slot, block[0:3], block[3:4], away_density, away_force, local)
        return carry

    lax.fori_loop(0, CODES, other, 0, unroll=3)

    unroll = 8

    def some(step, carry):
        for part in range(unroll):
            block = step * unroll + part
            left = home[block]
            names = [block] + [lookup[block, n] for n in range(NEIGHBOURS)]
            total = jnp.zeros((WIDTH, WIDTH), f32)
            for first in range(0, NEIGHBOURS + 1, 2):
                some_names = names[first : first + 2]
                right = jnp.concatenate([away_density[n] for n in some_names], axis=1)
                kernel = jnp.maximum(jnp.dot(left, right, preferred_element_type=f32), 0.0)
                cube = kernel * kernel * kernel
                for k in range(len(some_names)):
                    total = total + cube[:, k * WIDTH : (k + 1) * WIDTH]
            rho[pl.ds(block, 1)] = lane_sums(total)
        return carry

    lax.fori_loop(0, BLOCKS // unroll, some, 0)

    def one(code, carry):
        device = near_device(place, code)
        for slot in range(GHOST_CAP):
            row = jnp.maximum(send[device, slot], 0)
            rho_send[device, pl.ds(slot, 1)] = rho[pl.ds(row, 1)]
        return carry

    lax.fori_loop(0, CODES, one, 0)


def pressure(density):
    return jnp.exp(jnp.log(density) * (-1.0 / 3.0))


def force_kernel(place, lookup, rho, rho_ghosts, away_force, home, local, emit):
    terms = pressure(rho[...])
    for block in range(BLOCKS):
        local[block, 3:4] = terms[block : block + 1]

    def other(code, carry):
        device = near_device(place, code)
        values = pressure(rho_ghosts[device])
        for slot in range(GHOST_CAP):
            local[BLOCKS + code * GHOST_CAP + slot, 3:4] = values[slot : slot + 1]
        return carry

    lax.fori_loop(0, CODES, other, 0, unroll=3)

    unroll = 4

    def some(step, carry):
        for part in range(unroll):
            block = step * unroll + part
            left = home[block]
            mine = local[block]
            names = [block] + [lookup[block, n] for n in range(NEIGHBOURS)]
            own_term = jnp.broadcast_to(mine[3:4], (WIDTH, WIDTH)).T
            total = [jnp.zeros((WIDTH, WIDTH), f32) for _ in range(4)]
            for first in range(0, NEIGHBOURS + 1, 2):
                some_names = names[first : first + 2]
                right = jnp.concatenate([away_force[n] for n in some_names], axis=1)
                kernel = jnp.maximum(jnp.dot(left, right, preferred_element_type=f32), 0.0)
                for k, name in enumerate(some_names):
                    this = kernel[:, k * WIDTH : (k + 1) * WIDTH]
                    weight = this * this * (own_term + local[name, 3:4])
                    total[3] = total[3] + weight
                    for c in range(3):
                        total[c] = total[c] + weight * local[name, c : c + 1]
            whole = lane_sums(total[3])
            pull = [24.0 * (mine[c : c + 1] * whole - lane_sums(total[c])) for c in range(3)]
            emit(block, jnp.concatenate(pull, axis=0))
        return carry

    lax.fori_loop(0, BLOCKS // unroll, some, 0)


def merge_kernel(place, labels, send, stay, arrived, points, velocity, mass, ghost_send):
    def put(spot, rows):
        points[spot] = rows[0:3]
        velocity[spot] = rows[3:6]
        mass[pl.ds(spot, 1)] = rows[6:7]

    def copy(block, carry):
        put(block, stay[block])
        return carry

    lax.fori_loop(0, BLOCKS, copy, 0)
    for k in range(6 * MOVE_CAP):

        @pl.when(labels[k] > 0)
        def _():
            put(labels[k] - 1, arrived[k])

    def load(row):
        return jnp.concatenate([points[row], mass[pl.ds(row, 1)]], axis=0)

    fill_sends(place, send, ghost_send, load)


def pack_kernel(place, send, points, mass, ghost_send):
    def load(row):
        return jnp.concatenate([points[row], mass[pl.ds(row, 1)]], axis=0)

    fill_sends(place, send, ghost_send, load)


def last_force_kernel(place, lookup, rho, rho_ghosts, away_force, home, local_in, points, velocity, points_out, velocity_out, local):
    local[...] = local_in[...]

    def emit(block, pull):
        speed = velocity[block] + time_step * pull
        velocity_out[block] = speed
        points_out[block] = points[block] + time_step * speed

    force_kernel(place, lookup, rho, rho_ghosts, away_force, home, local, emit)


def table_rows(neighbours):
    size_y = lax.axis_size("gy")
    size_z = lax.axis_size("gz")
    remote = jnp.maximum(neighbours - BLOCKS, 0)
    source = remote // GHOST_CAP
    within = remote % GHOST_CAP
    code = (source // (size_y * size_z) - lax.axis_index("gx") + 1) * 9
    code = code + (source // size_z % size_y - lax.axis_index("gy") + 1) * 3
    code = code + (source % size_z - lax.axis_index("gz") + 1)
    return jnp.where(neighbours < BLOCKS, neighbours, BLOCKS + code * GHOST_CAP + within)


def goals(destination):
    size_y = lax.axis_size("gy")
    size_z = lax.axis_size("gz")
    device = destination // BLOCKS
    place = destination % BLOCKS
    moving = device != lax.axis_index(AXES)
    dx = device // (size_y * size_z) - lax.axis_index("gx")
    dy = device // size_z % size_y - lax.axis_index("gy")
    dz = device % size_z - lax.axis_index("gz")
    heading = jnp.where(
        dx != 0,
        (dx > 0).astype(jnp.int32),
        jnp.where(dy != 0, 2 + (dy > 0).astype(jnp.int32), 4 + (dz > 0).astype(jnp.int32)),
    )
    heading = jnp.where(moving, heading, -1)
    number = jnp.arange(BLOCKS, dtype=jnp.int32)
    before = (heading[:, None] == heading[None, :]) & (number[None, :] < number[:, None])
    used = jnp.minimum(jnp.sum(before.astype(jnp.int32), axis=1), MOVE_CAP - 1)
    return jnp.where(moving, BLOCKS + heading * MOVE_CAP + used, place), place + 1


def to_all(values):
    return lax.all_to_all(values, AXES, 0, 0, tiled=True)


def shifted(values, axis, step):
    count = lax.axis_size(axis)
    pairs = [(i, i + step) for i in range(count) if 0 <= i + step < count]
    return lax.ppermute(values, axis, pairs)


def densities(place, lookup, send, points, mass, ghost_send, devices):
    ghosts = to_all(ghost_send)
    own_density, own_force, home, own_local = call(
        own_kernel,
        "own",
        [SMEM] + [VMEM] * 2,
        [
            shape(BLOCKS, TERMS, WIDTH, dtype=bf16),
            shape(BLOCKS, TERMS, WIDTH, dtype=bf16),
            shape(BLOCKS, WIDTH, TERMS, dtype=bf16),
            shape(BLOCKS, 8, WIDTH),
        ],
        cost=(10_000_000_000, 8_000_000),
    )(place, points, mass)
    rho, rho_send, away_force, local = call(
        density_kernel,
        "density",
        [SMEM] * 3 + [VMEM] * 5,
        [
            shape(BLOCKS, WIDTH),
            shape(devices, GHOST_CAP, WIDTH),
            shape(STORED, TERMS, WIDTH, dtype=bf16),
            shape(STORED, 8, WIDTH),
        ],
        [pltpu.VMEM((STORED, TERMS, WIDTH), bf16)],
        cost=(80_000_000_000, 8_000_000),
    )(place, lookup, send, ghosts, own_density, own_force, home, own_local)
    return rho, rho_send, away_force, home, local


def per_device(position, velocity, mass, send_first, neighbours_first, destination, send_second, neighbours_second):
    sizes = [lax.axis_size(a) for a in AXES]
    devices = sizes[0] * sizes[1] * sizes[2]
    place = jnp.stack(
        [lax.axis_index(AXES).astype(jnp.int32)]
        + [lax.axis_index(a).astype(jnp.int32) for a in AXES]
        + [jnp.int32(s) for s in sizes]
    )
    send_first, send_second = send_first[0], send_second[0]
    lookup_first, lookup_second = table_rows(neighbours_first), table_rows(neighbours_second)
    ghost_shape = shape(devices, GHOST_CAP, 4, WIDTH)
    ghost_send = call(pack_kernel, "pack", [SMEM] * 2 + [VMEM] * 2, ghost_shape)(place, send_first, position, mass)
    rho, rho_send, away_force, home, local = densities(
        place, lookup_first, send_first, position, mass, ghost_send, devices
    )
    rho_ghosts = to_all(rho_send)

    slots, marks = goals(destination)

    def first(place, lookup, slots, marks, rho, rho_ghosts, away_force, home, local_in, points, velocity, mass, state, local):
        local[...] = local_in[...]
        state[BLOCKS:] = jnp.zeros((6 * MOVE_CAP, 8, WIDTH), f32)

        def emit(block, pull):
            speed = velocity[block] + time_step * pull
            mark = jnp.full((1, WIDTH), marks[block], jnp.int32).astype(f32)
            rows = [points[block] + time_step * speed, speed, mass[pl.ds(block, 1)], mark]
            state[slots[block]] = jnp.concatenate(rows, axis=0)

        force_kernel(place, lookup, rho, rho_ghosts, away_force, home, local, emit)

    state = call(
        first,
        "force",
        [SMEM] * 4 + [VMEM] * 8,
        shape(BLOCKS + 6 * MOVE_CAP, 8, WIDTH),
        [pltpu.VMEM((STORED, 8, WIDTH), f32)],
    )(place, lookup_first, slots, marks, rho, rho_ghosts, away_force, home, local, position, velocity, mass)
    outbox = state[BLOCKS:]
    boxes = outbox.reshape(6, MOVE_CAP, 8, WIDTH)
    arrived = jnp.concatenate(
        [shifted(boxes[2 * k + way], axis, 2 * way - 1) for k, axis in enumerate(AXES) for way in (0, 1)], axis=0
    )
    labels = arrived[:, 7, 0].astype(jnp.int32)
    position, velocity, mass, ghost_send = call(
        merge_kernel,
        "merge",
        [SMEM] * 3 + [VMEM] * 2,
        [shape(BLOCKS, 3, WIDTH), shape(BLOCKS, 3, WIDTH), shape(BLOCKS, WIDTH), ghost_shape],
    )(place, labels, send_second, state, arrived)
    rho, rho_send, away_force, home, local = densities(
        place, lookup_second, send_second, position, mass, ghost_send, devices
    )
    rho_ghosts = to_all(rho_send)
    position, velocity = call(
        last_force_kernel,
        "last_force",
        [SMEM] * 2 + [VMEM] * 7,
        [shape(BLOCKS, 3, WIDTH), shape(BLOCKS, 3, WIDTH)],
        [pltpu.VMEM((STORED, 8, WIDTH), f32)],
    )(place, lookup_second, rho, rho_ghosts, away_force, home, local, position, velocity)
    return position, velocity, rho


def solution(mesh):
    along = P(AXES)
    return jax.shard_map(
        per_device, mesh=mesh, in_specs=(along,) * 8, out_specs=(along,) * 3, check_vma=False
    )
```
